512 devices in a mesh: dp: 64 (over x, z_hi, y), tensor: 8 (over z_lo, core).
Axes of the slice: x: 4, y: 4, z: 16 (z_hi: 4, z_lo: 4; z = z_hi * 4 + z_lo), core: 2. Of those that a mesh axis runs over, the one named last changes fastest.
Arguments:
- inputs: bfloat16 [32768, 6144], P('dp', 'tensor'), may hold values from -16 to 16
- expert_ids: int32 [32768, 2], P('dp'), may hold values from 0 to 7, as said below
- hidden_grads: bfloat16 [32768, 2, 16384], P('dp', None, 'tensor'), may hold values from -42 to 42
- input_probes: bfloat16 [6144, 48], P('tensor'), may hold values from -6 to 6
- hidden_probes: bfloat16 [16384, 32], P('tensor'), may hold values from -6 to 6
Outputs:
- input_sketch: float32 [6144, 384], P(('tensor', 'dp'))
- hidden_sketch: float32 [16384, 256], P(('tensor', 'dp'))
The draws below stay inside these ranges and needn't reach their ends.
Inputs may be any that keep to these rules, and one draw needn't show every extreme that they name: `expert_ids`: the 2 experts of a token differ; every expert is named by some token.
All inputs are finite; a program needn't handle non-finite values.
Results may differ from the reference program's by a relative error of at most 0.0024.
Values sent between devices are 32-bit elements; how exact they have to be, the bound alone decides.
No kernel may reach another device: no remote copies, remote signals or barrier semaphores. Data moves between devices by JAX's collectives and lax.ppermute only.
A program may use at most 64 MiB of HBM per device.

```python
import math
import jax
import jax.numpy as jnp
from jax import lax

D = 6144
FF = 16384
EXPERTS = 8
TOP = 2
PROBES = 48
HPROBES = 32
TOKENS = 32768
N_TENSOR = 8


def draw_expert_ids(key, part):
    key = jax.random.fold_in(key, 11)
    first_key, second_key, third_key = jax.random.split(key, 3)
    fourth_key = jax.random.fold_in(key, 5)
    positions = jnp.arange(TOKENS, dtype=jnp.int32)
    home = positions * EXPERTS // TOKENS
    coin = jax.random.randint(first_key, (TOKENS,), 0, 2)
    other = jax.random.randint(second_key, (TOKENS,), 0, EXPERTS)
    leading = positions % (TOKENS // EXPERTS) == 0
    first = jnp.where((coin == 0) | leading, home, other)
    offset = jax.random.randint(third_key, (TOKENS,), 1, EXPERTS)
    second = (first + offset) % EXPERTS
    swap_coin = jax.random.randint(fourth_key, (TOKENS,), 0, 2)
    left = jnp.where(swap_coin == 0, first, second)
    right = jnp.where(swap_coin == 0, second, first)
    return jnp.stack([left, right], axis=1).astype(jnp.int32)


def draw_hidden_grads(key, part):
    key = jax.random.fold_in(key, 7)
    first_key, second_key = jax.random.split(key, 2)
    values = jnp.clip(jax.random.normal(first_key, (TOKENS, TOP, FF), jnp.float32), -6.0, 6.0)
    rows = jnp.exp(jax.random.uniform(second_key, (TOKENS, TOP, 1), jnp.float32, -1.38, 1.38))
    ramp = 1.0 + 0.75 * jnp.arange(FF, dtype=jnp.float32) / FF
    return (values * rows * ramp).astype(jnp.bfloat16)


def strengthened(values, key, source, target, blocks, factor):
    owner, partner = [(jnp.arange(values.shape[dim]) // (values.shape[dim] // blocks)).reshape([-1 if axis == dim else 1 for axis in range(values.ndim)]) for dim in (source, target)]
    chosen = jax.random.permutation(key, blocks)[partner]
    strong = (owner == chosen) | (owner == (partner + blocks // 2) % blocks)
    return jnp.where(strong, factor * values, values)


def block_scale(stream_key, shape, pieces, least, top_value):
    gain = 1.0
    for dim, parts in pieces:
        steps = jax.random.uniform(jax.random.fold_in(jax.random.fold_in(stream_key, 6), dim), (parts,), jnp.float32, least / len(pieces), top_value / len(pieces))
        gain = gain * jnp.repeat(jnp.exp(steps), shape[dim] // parts).reshape((-1,) + (1,) * (len(shape) - 1 - dim))
    return gain


def centred(key, shape, spread, bound, shards=(), held_as=jnp.bfloat16):
    array = spread * jax.random.normal(key, shape, jnp.float32)
    if shards:
        array = array * block_scale(key, shape, shards, -0.22, 0.18)
    return jnp.clip(array, -bound, bound).astype(held_as)


def noise_with(key, dims, spread, most, pieces, heavy, held_as=jnp.bfloat16):
    entries = spread * jax.random.normal(key, dims, jnp.float32)
    if pieces:
        entries = entries * block_scale(key, dims, pieces, -0.22, 0.18)
    return jnp.clip(strengthened(entries, jax.random.fold_in(key, 3), *heavy), -most, most).astype(held_as)


def setup_inputs(seed: int = 0) -> dict:
    streams_of = jax.random.split(jax.random.key(seed), 6)
    inputs = noise_with(streams_of[0], (TOKENS, D), 1.0, 16.0, ((0, 64), (1, 8)), (0, 1, 64, 4.0))
    expert_ids = draw_expert_ids(jax.random.fold_in(streams_of[5], 71), 0)
    hidden_grads = draw_hidden_grads(jax.random.fold_in(streams_of[5], 71), 0)
    input_probes = centred(streams_of[3], (D, PROBES), 1.0, 6.0, ((0, 8),))
    hidden_probes = centred(streams_of[4], (FF, HPROBES), 1.0, 6.0, ((0, 8),))
    return {"inputs": inputs, "expert_ids": expert_ids, "hidden_grads": hidden_grads, "input_probes": input_probes, "hidden_probes": hidden_probes}


EPS = 1e-06

def contract(left, right):
    return lax.dot_general(left, right, (((0,), (0,)), ((), ())), preferred_element_type=jnp.float32)

def reference(inputs, expert_ids, hidden_grads, input_probes, hidden_probes):
    experts = jnp.arange(EXPERTS, dtype=jnp.int32)
    onehot = (expert_ids[:, :, None] == experts).astype(jnp.int32)
    routed = lax.optimization_barrier(jnp.sum(onehot, axis=1))
    counts = lax.optimization_barrier(jnp.sum(routed, axis=0)).astype(jnp.float32)
    projected = jnp.dot(inputs, input_probes, preferred_element_type=jnp.float32)
    weighted = (routed.astype(jnp.float32)[:, :, None] * projected[:, None, :]).astype(jnp.bfloat16)
    weighted = weighted.reshape(TOKENS, EXPERTS * PROBES)
    input_sketch = contract(inputs, weighted) / jnp.repeat(counts, PROBES)[None, :]
    fslice = FF // N_TENSOR
    squares = jnp.zeros((TOKENS, TOP), jnp.float32)
    for index in range(N_TENSOR):
        block = hidden_grads[:, :, index * fslice:(index + 1) * fslice].astype(jnp.float32)
        squares = squares + lax.optimization_barrier(jnp.sum(block * block, axis=2))
    scale = jnp.minimum(1.0, math.sqrt(FF) * lax.rsqrt(squares + EPS))
    route_flat = onehot.reshape(TOKENS * TOP, EXPERTS).astype(jnp.float32)
    hblocks = []
    for index in range(N_TENSOR):
        block = hidden_grads[:, :, index * fslice:(index + 1) * fslice].astype(jnp.float32)
        clipped = (block * scale[:, :, None]).astype(jnp.bfloat16).reshape(TOKENS * TOP, fslice)
        hprojected = jnp.dot(clipped, hidden_probes[index * fslice:(index + 1) * fslice], preferred_element_type=jnp.float32)
        hweighted = (route_flat[:, :, None] * hprojected[:, None, :]).astype(jnp.bfloat16)
        hweighted = hweighted.reshape(TOKENS * TOP, EXPERTS * HPROBES)
        hblocks.append(contract(clipped, hweighted))
    hidden_sketch = jnp.concatenate(hblocks, axis=0) / jnp.repeat(counts, HPROBES)[None, :]
    return (input_sketch, hidden_sketch)
```

```python
import jax
import jax.numpy as jnp
from jax import lax
from jax.sharding import PartitionSpec as P

FF = 16384
EXPERTS = 8
PROBES = 48
HPROBES = 32
EPS = 1e-06
AXES = ("dp", "tensor")


def linear(x, zh, y, t):
    return ((x * 4 + zh) * 4 + y) * 8 + t


def ring_groups(first):
    groups = []
    for zh in range(4):
        for t in range(8):
            along_x = (t % 2 == 0) == first
            for other in range(4):
                groups.append(
                    [linear(i, zh, other, t) if along_x else linear(other, zh, i, t) for i in range(4)]
                )
    return groups


def zh_groups():
    return [
        [linear(x, zh, y, t) for zh in range(4)] for x in range(4) for y in range(4) for t in range(8)
    ]


def exchange(block, groups):
    got = lax.all_to_all(block, AXES, 0, 0, axis_index_groups=groups)
    return jnp.sum(got, axis=0)


def contract(left, right, dims):
    return lax.dot_general(left, right, (dims, ((), ())), preferred_element_type=jnp.float32)


def body(inputs, expert_ids, hidden_grads, input_probes, hidden_probes):
    tokens = inputs.shape[0]
    width = hidden_grads.shape[2]
    experts = jnp.arange(EXPERTS, dtype=jnp.int32)
    onehot = (expert_ids[:, :, None] == experts).astype(jnp.float32)
    routed = jnp.sum(onehot, axis=1)
    local_counts = jnp.sum(routed, axis=0)

    grads_wide = hidden_grads.astype(jnp.float32)
    local_squares = jnp.sum(grads_wide * grads_wide, axis=2)
    partial_proj = contract(input_probes, inputs, ((0,), (1,)))
    hproj = contract(hidden_grads, hidden_probes, ((2,), (0,)))

    send = jnp.concatenate(
        [
            partial_proj.reshape(8, 6, tokens),
            jnp.broadcast_to(local_squares.T[None], (8, 2, tokens)),
        ],
        axis=1,
    )
    mine = jnp.sum(lax.all_to_all(send, "tensor", 0, 0), axis=0)
    squares = mine[6:].T
    everyone = lax.all_to_all(jnp.broadcast_to(mine[None], (8, 8, tokens)), "tensor", 0, 0)
    projected = everyone[:, :6].reshape(PROBES, tokens).T

    weighted = (routed[:, :, None] * projected[:, None, :]).astype(jnp.bfloat16)
    weighted = weighted.reshape(tokens, EXPERTS * PROBES)
    square_scale = jnp.minimum(1.0, FF / (squares + EPS))
    hweighted = (onehot[:, :, :, None] * (square_scale[:, :, None] * hproj)[:, :, None, :]).astype(
        jnp.bfloat16
    )
    hweighted = hweighted.reshape(tokens, 2, EXPERTS * HPROBES)
    hidden = contract(hidden_grads, hweighted, ((0, 1), (0, 1)))
    inp = contract(inputs, weighted, ((0,), (0,)))

    hidden = hidden.reshape(64, width // 64, 2, 128).transpose(0, 2, 1, 3).reshape(64, 64, 128)
    inp = inp.reshape(64, 12, 3, 128).transpose(0, 2, 1, 3).reshape(64, 36, 128)
    count_rows = jnp.broadcast_to(jnp.pad(local_counts, (0, 120)), (64, 4, 128))
    block = jnp.concatenate([hidden, inp, count_rows], axis=1).reshape(4, 4, 4, 104, 128)
    even = lax.axis_index("tensor") % 2 == 0
    block = jnp.where(even, block.transpose(0, 2, 1, 3, 4), block.transpose(2, 0, 1, 3, 4))
    block = exchange(block, ring_groups(True))
    block = exchange(block, ring_groups(False))
    block = exchange(block, zh_groups())

    counts = block[100, :8]
    hidden = jnp.concatenate([block[:32], block[32:64]], axis=1)
    inp = jnp.concatenate([block[64:76], block[76:88], block[88:100]], axis=1)
    return (
        inp / jnp.repeat(counts, PROBES)[None, :],
        hidden / jnp.repeat(counts, HPROBES)[None, :],
    )


def solution(mesh):
    return jax.shard_map(
        body,
        mesh=mesh,
        in_specs=(
            P("dp", "tensor"),
            P("dp", None),
            P("dp", None, "tensor"),
            P("tensor", None),
            P("tensor", None),
        ),
        out_specs=(P(("tensor", "dp"), None), P(("tensor", "dp"), None)),
        check_vma=False,
    )
```

```python
import functools

import jax
import jax.numpy as jnp
from jax import lax
from jax.experimental import pallas as pl
from jax.experimental.pallas import tpu as pltpu
from jax.sharding import PartitionSpec as P

FF = 16384
EXPERTS = 8
PROBES = 48
HPROBES = 32
EPS = 1e-06
AXES = ("dp", "tensor")
PARAMS = pltpu.CompilerParams(vmem_limit_bytes=40 * 1024 * 1024)
VMEM = pl.BlockSpec(memory_space=pltpu.VMEM)
SMEM = pl.BlockSpec(memory_space=pltpu.SMEM)


def linear(x, zh, y, t):
    return ((x * 4 + zh) * 4 + y) * 8 + t


def ring_groups(first):
    groups = []
    for zh in range(4):
        for t in range(8):
            along_x = (t % 2 == 0) == first
            for other in range(4):
                groups.append(
                    [linear(i, zh, other, t) if along_x else linear(other, zh, i, t) for i in range(4)]
                )
    return groups


def zh_groups():
    return [
        [linear(x, zh, y, t) for zh in range(4)] for x in range(4) for y in range(4) for t in range(8)
    ]


def swap(block, groups):
    return lax.all_to_all(block, AXES, 0, 0, axis_index_groups=groups)


def nt(left, right, **kw):
    return lax.dot_general(
        left, right, (((1,), (1,)), ((), ())), preferred_element_type=jnp.float32, **kw
    )


def first_kernel(grads_ref, inputs_ref, hprobes_ref, probes_ref, send_ref, hproj_ref):
    ones = jnp.ones((8, 128), jnp.float32)
    for b in range(4):
        rows = grads_ref[256 * b : 256 * (b + 1)]
        wide = rows.astype(jnp.float32)
        part = jnp.zeros((256, 128), jnp.float32)
        for i in range(16):
            piece = wide[:, 128 * i : 128 * (i + 1)]
            part = part + piece * piece
        squares = nt(ones, part, precision=lax.Precision.HIGHEST)
        hproj_ref[:, 256 * b : 256 * (b + 1)] = nt(hprobes_ref[...], rows)
        proj = nt(probes_ref[...], inputs_ref[128 * b : 128 * (b + 1)])
        lanes = 256 * (b % 2)
        for t in range(8):
            send_ref[t, 0:6, 128 * b : 128 * (b + 1)] = proj[6 * t : 6 * t + 6]
            send_ref[t, 6 + b // 2, lanes : lanes + 256] = squares[0]


def hidden_kernel(place_ref, got_ref, hproj_ref, ids_ref, grads_ref, out_ref):
    got = jnp.sum(got_ref[...], axis=0)
    squares = jnp.concatenate([got[6:7], got[7:8]], axis=1)
    scaled = hproj_ref[...] * jnp.minimum(1.0, FF / (squares + EPS))
    ids = ids_ref[...]
    weights = jnp.concatenate(
        [jnp.where(ids == e, scaled, 0.0).astype(jnp.bfloat16) for e in range(EXPERTS)], axis=0
    )
    rows = grads_ref[...]
    for b in range(8):
        product = jnp.dot(
            weights, rows[:, 256 * b : 256 * (b + 1)], preferred_element_type=jnp.float32
        ).T
        for c in range(8):
            out_ref[place_ref[8 * b + c]] = product[32 * c : 32 * c + 32]


def input_kernel(core_ref, everyone_ref, ids_ref, inputs_ref, out_ref):
    projected = jnp.concatenate([everyone_ref[t, 0:6] for t in range(8)], axis=0)
    ids = ids_ref[...]
    routed = [(ids[0:1] == e) | (ids[1:2] == e) for e in range(EXPERTS)]
    weights = jnp.concatenate(
        [jnp.where(r, projected, 0.0).astype(jnp.bfloat16) for r in routed], axis=0
    )
    product = jnp.dot(weights, inputs_ref[...], preferred_element_type=jnp.float32).T

    def marks(repeat, total):
        marked = [
            jnp.broadcast_to(jnp.where(r, 1.0, 0.0).astype(jnp.bfloat16), (repeat, r.shape[1]))
            for r in routed
        ]
        marked = jnp.concatenate(marked, axis=0)
        return nt(jnp.ones((8, r_tokens), jnp.bfloat16), marked)

    r_tokens = ids.shape[1]
    for_inputs = marks(PROBES, 384)
    for_hidden = jnp.concatenate([marks(HPROBES, 256), jnp.zeros((8, 128), jnp.float32)], axis=1)
    counts = jnp.concatenate(
        [for_inputs[0:1], for_hidden[0:1], jnp.zeros((6, 384), jnp.float32)], axis=0
    )
    for i in range(4):
        out_ref[i, 192:200] = counts

    def write(order):
        for x in range(4):
            for zh in range(4):
                for y in range(4):
                    start = ((x * 4 + zh) * 4 + y) * 12
                    major, minor = (x, y) if order else (y, x)
                    at = minor * 48 + zh * 12
                    out_ref[major, at : at + 12] = product[start : start + 12]

    pl.when(core_ref[0] == 0)(functools.partial(write, True))
    pl.when(core_ref[0] == 1)(functools.partial(write, False))


def last_kernel(hidden_ref, input_ref, input_out, hidden_out):
    total = jnp.sum(input_ref[...], axis=0)
    input_out[...] = total[0:12] / total[12:13]
    hidden_out[...] = jnp.sum(hidden_ref[...], axis=0) / total[13:14, :256]


def call(kernel, out_shape, in_specs, out_specs, flops, size):
    return pl.pallas_call(
        kernel,
        out_shape=out_shape,
        in_specs=in_specs,
        out_specs=out_specs,
        compiler_params=PARAMS,
        cost_estimate=pl.CostEstimate(flops=flops, bytes_accessed=size, transcendentals=0),
    )


def shape(*dims):
    return jax.ShapeDtypeStruct(dims, jnp.float32)


def body(inputs, expert_ids, hidden_grads, input_probes, hidden_probes):
    tokens = inputs.shape[0]
    core = lax.axis_index("tensor") % 2
    dp = jnp.arange(64, dtype=jnp.int32)
    x, zh, y = dp // 16, dp // 4 % 4, dp % 4
    place = jnp.where(core == 0, (x * 4 + y) * 4 + zh, (y * 4 + x) * 4 + zh)
    ids_pair = expert_ids.T
    hidden_grads = hidden_grads.reshape(2 * tokens, -1)
    ids_row = expert_ids.reshape(1, 2 * tokens)

    send, hproj = call(
        first_kernel, (shape(8, 8, tokens), shape(HPROBES, 2 * tokens)), [VMEM] * 4, (VMEM, VMEM), 10**9, 5 * 10**6
    )(hidden_grads, inputs, hidden_probes.T, input_probes.T)
    got = lax.all_to_all(send, "tensor", 0, 0)
    hidden = call(
        hidden_kernel, shape(64, 32, 256), [SMEM] + [VMEM] * 4, VMEM, 10**9, 6 * 10**6
    )(place, got, hproj, ids_row, hidden_grads)
    hidden = swap(hidden.reshape(4, 16, 32, 256), ring_groups(True))

    mine = jnp.sum(got, axis=0)
    everyone = lax.all_to_all(jnp.broadcast_to(mine[None], (8, 8, tokens)), "tensor", 0, 0)
    inp = call(
        input_kernel, shape(4, 200, 384), [SMEM] + [VMEM] * 3, VMEM, 10**9, 3 * 10**6
    )(core.reshape(1), everyone, ids_pair, inputs)
    inp = swap(inp, ring_groups(True))

    hidden = swap(jnp.sum(hidden, axis=0).reshape(4, 4, 32, 256), ring_groups(False))
    inp = jnp.sum(inp, axis=0)
    counts = jnp.broadcast_to(inp[192:], (4, 8, 384))
    inp = swap(jnp.concatenate([inp[:192].reshape(4, 48, 384), counts], axis=1), ring_groups(False))

    hidden = swap(jnp.sum(hidden, axis=0), zh_groups())
    inp = jnp.sum(inp, axis=0)
    counts = jnp.broadcast_to(inp[48:52], (4, 4, 384))
    inp = swap(jnp.concatenate([inp[:48].reshape(4, 12, 384), counts], axis=1), zh_groups())
    return call(
        last_kernel, (shape(12, 384), shape(32, 256)), [VMEM] * 2, (VMEM, VMEM), 10**5, 10**5
    )(hidden, inp)


def solution(mesh):
    return jax.shard_map(
        body,
        mesh=mesh,
        in_specs=(
            P("dp", "tensor"),
            P("dp", None),
            P("dp", None, "tensor"),
            P("tensor", None),
            P("tensor", None),
        ),
        out_specs=(P(("tensor", "dp"), None), P(("tensor", "dp"), None)),
        check_vma=False,
    )
```

```python
import jax
import jax.numpy as jnp
from jax import lax
from jax.experimental import pallas as pl
from jax.experimental.pallas import tpu as pltpu
from jax.sharding import PartitionSpec as P

FF = 16384
EXPERTS = 8
PROBES = 48
HPROBES = 32
EPS = 1e-06
AXES = ("dp", "tensor")
PARAMS = pltpu.CompilerParams(vmem_limit_bytes=40 * 1024 * 1024)
VMEM = pl.BlockSpec(memory_space=pltpu.VMEM)
SMEM = pl.BlockSpec(memory_space=pltpu.SMEM)


def linear(x, zh, y, t):
    return ((x * 4 + zh) * 4 + y) * 8 + t


def ring_groups(first):
    groups = []
    for zh in range(4):
        for t in range(8):
            along_x = (t % 2 == 0) == first
            for other in range(4):
                groups.append(
                    [linear(i, zh, other, t) if along_x else linear(other, zh, i, t) for i in range(4)]
                )
    return groups


def zh_groups():
    return [
        [linear(x, zh, y, t) for zh in range(4)] for x in range(4) for y in range(4) for t in range(8)
    ]


def swap(block, groups):
    return lax.all_to_all(block, AXES, 0, 0, axis_index_groups=groups)


def nt(left, right, **kw):
    return lax.dot_general(
        left, right, (((1,), (1,)), ((), ())), preferred_element_type=jnp.float32, **kw
    )


def projection_kernel(inputs_ref, probes_ref, send_ref):
    proj = nt(probes_ref[...], inputs_ref[...])
    for t in range(8):
        send_ref[t, 0:6] = proj[6 * t : 6 * t + 6]
        send_ref[t, 6:8] = jnp.zeros_like(send_ref[t, 6:8])


def order_matrix():
    row = lax.broadcasted_iota(jnp.int32, (256, 256), 0)
    column = lax.broadcasted_iota(jnp.int32, (256, 256), 1)
    source = ((row >> 1) & 7) * 32 + (row >> 4) * 2 + (row & 1)
    return jnp.where(column == source, 1.0, 0.0).astype(jnp.bfloat16)


def grads_kernel(view_ref, hprobes_ref, rows_ref, hproj_ref, squares_ref, part_ref):
    order = order_matrix()

    def step(i, carry):
        for half in range(2):
            first = i * 4 + half * 2
            pair = jnp.concatenate(
                [view_ref[pl.ds((first + m) * 8, 8)].reshape(256, 128) for m in range(2)], axis=1
            )
            ordered = jnp.dot(order, pair, preferred_element_type=jnp.float32)
            for m in range(2):
                at = pl.multiple_of((first + m) * 16, 16)
                part = jnp.zeros((16, 128), jnp.float32)
                for tile in range(16):
                    piece = ordered[16 * tile : 16 * tile + 16, 128 * m : 128 * (m + 1)]
                    part = part + piece * piece
                    rows_ref[pl.ds(at, 16), 128 * tile : 128 * (tile + 1)] = piece.astype(jnp.bfloat16)
                part_ref[pl.ds(at, 16)] = part
        return carry

    lax.fori_loop(0, 16, step, 0)
    squares = nt(jnp.ones((8, 128), jnp.float32), part_ref[...], precision=lax.Precision.HIGHEST)
    squares_ref[0:1] = squares[0:1, 0:512]
    squares_ref[1:2] = squares[0:1, 512:1024]
    hproj_ref[...] = nt(hprobes_ref[...], rows_ref[...])


def between_kernel(got_ref, squares_ref, send_ref):
    mine = jnp.sum(got_ref[...], axis=0)
    for t in range(8):
        send_ref[t, 0:6] = mine[0:6]
        send_ref[t, 6:8] = squares_ref[...]


def hidden_kernel(place_ref, got_ref, hproj_ref, ids_ref, rows_ref, out_ref):
    got = jnp.sum(got_ref[...], axis=0)
    squares = jnp.concatenate([got[6:7], got[7:8]], axis=1)
    scaled = hproj_ref[...] * jnp.minimum(1.0, FF / (squares + EPS))
    ids = ids_ref[...]
    weights = jnp.concatenate(
        [jnp.where(ids == e, scaled, 0.0).astype(jnp.bfloat16) for e in range(EXPERTS)], axis=0
    )
    rows = rows_ref[...]
    for b in range(8):
        product = jnp.dot(
            weights, rows[:, 256 * b : 256 * (b + 1)], preferred_element_type=jnp.float32
        ).T
        for c in range(8):
            place = place_ref[8 * b + c]
            out_ref[place, 0:32] = product[32 * c : 32 * c + 32, 0:128]
            out_ref[place, 32:64] = product[32 * c : 32 * c + 32, 128:256]


def input_kernel(place_ref, everyone_ref, ids_ref, inputs_ref, partly_ref, out_ref):
    del partly_ref
    projected = jnp.concatenate([everyone_ref[t, 0:6] for t in range(8)], axis=0)
    ids = ids_ref[...]
    routed = [(ids[0:1] == e) | (ids[1:2] == e) for e in range(EXPERTS)]
    weights = jnp.concatenate(
        [jnp.where(r, projected, 0.0).astype(jnp.bfloat16) for r in routed], axis=0
    )
    product = jnp.dot(weights, inputs_ref[...], preferred_element_type=jnp.float32).T
    lane = lax.broadcasted_iota(jnp.int32, (4, 128), 1)
    counts = jnp.zeros((4, 128), jnp.float32)
    for e in range(EXPERTS):
        total = jnp.sum(jnp.where(routed[e], 1.0, 0.0), axis=1, keepdims=True)
        counts = jnp.where(lane == e, total, counts)
    for d in range(64):
        place = place_ref[d]
        for m in range(3):
            out_ref[place, 64 + 12 * m : 76 + 12 * m] = product[
                12 * d : 12 * d + 12, 128 * m : 128 * (m + 1)
            ]
        out_ref[place, 100:104] = counts


def last_kernel(block_ref, input_out, hidden_out):
    total = jnp.sum(block_ref[...], axis=0)
    for out, first, rows, tiles, repeat in (
        (input_out, 64, 12, 3, PROBES),
        (hidden_out, 0, 32, 2, HPROBES),
    ):
        for m in range(tiles):
            owner = (lax.broadcasted_iota(jnp.int32, (1, 128), 1) + 128 * m) // repeat
            counts = jnp.zeros((1, 128), jnp.float32)
            for e in range(EXPERTS):
                counts = jnp.where(owner == e, total[100:101, e : e + 1], counts)
            out[:, 128 * m : 128 * (m + 1)] = total[first + rows * m : first + rows * (m + 1)] / counts


def call(kernel, out_shape, in_specs, out_specs, flops, size, **kw):
    return pl.pallas_call(
        kernel,
        out_shape=out_shape,
        in_specs=in_specs,
        out_specs=out_specs,
        compiler_params=PARAMS,
        cost_estimate=pl.CostEstimate(flops=flops, bytes_accessed=size, transcendentals=0),
        **kw,
    )


def shape(*dims):
    return jax.ShapeDtypeStruct(dims, jnp.float32)


def body(inputs, expert_ids, hidden_grads, input_probes, hidden_probes):
    tokens = inputs.shape[0]
    core = lax.axis_index("tensor") % 2
    dp = jnp.arange(64, dtype=jnp.int32)
    x, zh, y = dp // 16, dp // 4 % 4, dp % 4
    place = jnp.where(core == 0, (x * 4 + y) * 4 + zh, (y * 4 + x) * 4 + zh)
    ids_pair = expert_ids.T
    ids_row = expert_ids.reshape(1, 2 * tokens)

    send = call(projection_kernel, shape(8, 8, tokens), [VMEM] * 2, VMEM, 10**8, 10**6)(
        inputs, input_probes.T
    )
    got = lax.all_to_all(send, "tensor", 0, 0)
    view = hidden_grads.reshape(tokens, 2, 16, 128).transpose(0, 2, 1, 3).reshape(tokens, 32, 128)
    rows, hproj, squares = call(
        grads_kernel,
        (
            jax.ShapeDtypeStruct((2 * tokens, 2048), jnp.bfloat16),
            shape(HPROBES, 2 * tokens),
            shape(2, tokens),
        ),
        [VMEM] * 2,
        (VMEM,) * 3,
        4 * 10**9,
        9 * 10**6,
        scratch_shapes=[pltpu.VMEM((2 * tokens, 128), jnp.float32)],
    )(view, hidden_probes.T)
    send = call(between_kernel, shape(8, 8, tokens), [VMEM] * 2, VMEM, 10**5, 10**5)(got, squares)
    everyone = lax.all_to_all(send, "tensor", 0, 0)
    block = call(
        hidden_kernel, shape(64, 104, 128), [SMEM] + [VMEM] * 4, VMEM, 10**9, 6 * 10**6
    )(place, everyone, hproj, ids_row, rows)
    block = call(
        input_kernel,
        shape(64, 104, 128),
        [SMEM] + [VMEM] * 4,
        VMEM,
        10**9,
        3 * 10**6,
        input_output_aliases={4: 0},
    )(place, everyone, ids_pair, inputs, block)
    block = jnp.sum(swap(block.reshape(4, 16, 104, 128), ring_groups(True)), axis=0)
    block = jnp.sum(swap(block.reshape(4, 4, 104, 128), ring_groups(False)), axis=0)
    block = swap(block, zh_groups())
    return call(
        last_kernel, (shape(12, 384), shape(32, 256)), [VMEM], (VMEM, VMEM), 10**5, 10**5
    )(block)


def solution(mesh):
    return jax.shard_map(
        body,
        mesh=mesh,
        in_specs=(
            P("dp", "tensor"),
            P("dp", None),
            P("dp", None, "tensor"),
            P("tensor", None),
            P("tensor", None),
        ),
        out_specs=(P(("tensor", "dp"), None), P(("tensor", "dp"), None)),
        check_vma=False,
    )
```

```python
import jax
import jax.numpy as jnp
from jax import lax
from jax.experimental import pallas as pl
from jax.experimental.pallas import tpu as pltpu
from jax.sharding import PartitionSpec as P

FF = 16384
EXPERTS = 8
PROBES = 48
HPROBES = 32
EPS = 1e-06
AXES = ("dp", "tensor")
LIMIT = 40 * 10**6
VMEM = pl.BlockSpec(memory_space=pltpu.VMEM)
SMEM = pl.BlockSpec(memory_space=pltpu.SMEM)
HBM = pl.BlockSpec(memory_space=pltpu.HBM)
DMA = pltpu.SemaphoreType.DMA


def linear(x, zh, y, t):
    return ((x * 4 + zh) * 4 + y) * 8 + t


def ring_groups(first):
    groups = []
    for zh in range(4):
        for t in range(8):
            along_x = (t % 2 == 0) == first
            for other in range(4):
                groups.append(
                    [linear(i, zh, other, t) if along_x else linear(other, zh, i, t) for i in range(4)]
                )
    return groups


def zh_groups():
    return [
        [linear(x, zh, y, t) for zh in range(4)] for x in range(4) for y in range(4) for t in range(8)
    ]


def swap(block, groups):
    return lax.all_to_all(block, AXES, 0, 0, axis_index_groups=groups)


def nt(left, right, **kw):
    return lax.dot_general(
        left, right, (((1,), (1,)), ((), ())), preferred_element_type=jnp.float32, **kw
    )


def pick_matrix():
    row = lax.broadcasted_iota(jnp.int32, (256, 64), 0)
    column = lax.broadcasted_iota(jnp.int32, (256, 64), 1)
    same = ((row >> 3) == (column >> 1)) & ((row & 1) == (column & 1))
    return jnp.where(same, 1.0, 0.0).astype(jnp.bfloat16)


def thirds(value):
    high = value.astype(jnp.bfloat16).astype(jnp.float32)
    middle = (value - high).astype(jnp.bfloat16).astype(jnp.float32)
    rest = value - high - middle
    return jnp.concatenate([high, middle, rest, jnp.zeros_like(value)], axis=0).astype(jnp.bfloat16)


def norm_kernel(view_hbm, inputs_hbm, probes_hbm, send_ref, view_ref, inputs_ref, probes_ref, sems):
    loads = [
        pltpu.make_async_copy(
            view_hbm.at[pl.ds(128 * c, 128)], view_ref.at[pl.ds(128 * c, 128)], sems.at[c]
        )
        for c in range(4)
    ]
    loads += [
        pltpu.make_async_copy(inputs_hbm, inputs_ref, sems.at[4]),
        pltpu.make_async_copy(probes_hbm, probes_ref, sems.at[5]),
    ]
    for load in loads:
        load.start()
    ones = jnp.ones((8, 128), jnp.bfloat16)
    sums = []
    for c in range(4):
        loads[c].wait()
        wide = view_ref[128 * c : 128 * c + 128].astype(jnp.float32)
        wide = wide * wide
        part = (wide[:, 0:8] + wide[:, 8:16]) + (wide[:, 16:24] + wide[:, 24:32])
        part = part.reshape(1024, 128)
        high = part.astype(jnp.bfloat16)
        low = (part - high.astype(jnp.float32)).astype(jnp.bfloat16)
        sums.append((nt(ones, high) + nt(ones, low))[0:1])
    lanes = thirds(jnp.concatenate(sums, axis=1))
    pick = pick_matrix()
    picked = [
        jnp.dot(lanes[:, 256 * b : 256 * (b + 1)], pick, preferred_element_type=jnp.float32)
        for b in range(16)
    ]
    picked = jnp.sum(jnp.concatenate(picked, axis=1), axis=0, keepdims=True)
    for t in range(8):
        send_ref[t, 6:7] = picked[:, 0:512]
        send_ref[t, 7:8] = picked[:, 512:1024]
    loads[4].wait()
    loads[5].wait()
    proj = nt(probes_ref[...], inputs_ref[...])
    for t in range(8):
        send_ref[t, 0:6] = proj[6 * t : 6 * t + 6]


def order_matrix():
    row = lax.broadcasted_iota(jnp.int32, (256, 256), 0)
    column = lax.broadcasted_iota(jnp.int32, (256, 256), 1)
    source = ((row >> 1) & 7) * 32 + (row >> 4) * 2 + (row & 1)
    return jnp.where(column == source, 1.0, 0.0).astype(jnp.bfloat16)


def grads_kernel(
    view_hbm, hprobes_hbm, rows_hbm, hproj_ref, view_ref, rows_ref, hprobes_ref, sems, out_sems
):
    loads = [
        pltpu.make_async_copy(
            view_hbm.at[pl.ds(128 * c, 128)], view_ref.at[pl.ds(128 * c, 128)], sems.at[c]
        )
        for c in range(4)
    ]
    probe_load = pltpu.make_async_copy(hprobes_hbm, hprobes_ref, sems.at[4])
    for load in loads:
        load.start()
    probe_load.start()
    order = order_matrix()
    stores = []
    for c in range(4):
        loads[c].wait()

        def step(i, carry):
            for half in range(4):
                first = i * 8 + half * 2
                pair = jnp.concatenate(
                    [view_ref[pl.ds((first + m) * 8, 8)].reshape(256, 128) for m in range(2)], axis=1
                )
                ordered = jnp.dot(order, pair, preferred_element_type=jnp.float32)
                for m in range(2):
                    at = pl.multiple_of((first + m) * 16, 16)
                    for tile in range(16):
                        piece = ordered[16 * tile : 16 * tile + 16, 128 * m : 128 * (m + 1)]
                        lanes = 128 * (tile % 2)
                        rows_ref[tile // 2, pl.ds(at, 16), lanes : lanes + 128] = piece.astype(
                            jnp.bfloat16
                        )
            return carry

        lax.fori_loop(2 * c, 2 * c + 2, step, 0)
        here = pl.ds(256 * c, 256)
        store = pltpu.make_async_copy(rows_ref.at[:, here], rows_hbm.at[:, here], out_sems.at[c])
        store.start()
        stores.append(store)
        if c == 0:
            probe_load.wait()
        total = jnp.zeros((HPROBES, 256), jnp.float32)
        for b in range(8):
            total = total + nt(
                hprobes_ref[:, 256 * b : 256 * (b + 1)], rows_ref[b, 256 * c : 256 * c + 256]
            )
        hproj_ref[:, 256 * c : 256 * c + 256] = total
    for store in stores:
        store.wait()


def between_kernel(got_ref, send_ref):
    mine = jnp.sum(got_ref[...], axis=0)
    for t in range(8):
        send_ref[t] = mine


def hidden_kernel(place_ref, got_ref, hproj_ref, ids_ref, rows_ref, out_ref):
    got = jnp.sum(got_ref[...], axis=0)
    squares = jnp.concatenate([got[6:7], got[7:8]], axis=1)
    scaled = hproj_ref[...] * jnp.minimum(1.0, FF / (squares + EPS))
    ids = ids_ref[...]
    weights = jnp.concatenate(
        [jnp.where(ids == e, scaled, 0.0).astype(jnp.bfloat16) for e in range(EXPERTS)], axis=0
    )
    for b in range(8):
        product = jnp.dot(
            weights, rows_ref[b], preferred_element_type=jnp.float32
        ).T
        for c in range(8):
            place = place_ref[8 * b + c]
            out_ref[place, 0:32] = product[32 * c : 32 * c + 32, 0:128]
            out_ref[place, 32:64] = product[32 * c : 32 * c + 32, 128:256]


def input_kernel(place_ref, everyone_ref, ids_ref, inputs_ref, partly_ref, out_ref):
    del partly_ref
    projected = jnp.concatenate([everyone_ref[t, 0:6] for t in range(8)], axis=0)
    ids = ids_ref[...]
    routed = [(ids[0:1] == e) | (ids[1:2] == e) for e in range(EXPERTS)]
    weights = jnp.concatenate(
        [jnp.where(r, projected, 0.0).astype(jnp.bfloat16) for r in routed], axis=0
    )
    product = jnp.dot(weights, inputs_ref[...], preferred_element_type=jnp.float32).T
    lane = lax.broadcasted_iota(jnp.int32, (4, 128), 1)
    counts = jnp.zeros((4, 128), jnp.float32)
    for e in range(EXPERTS):
        total = jnp.sum(jnp.where(routed[e], 1.0, 0.0), axis=1, keepdims=True)
        counts = jnp.where(lane == e, total, counts)
    for d in range(64):
        place = place_ref[d]
        for m in range(3):
            out_ref[place, 64 + 12 * m : 76 + 12 * m] = product[
                12 * d : 12 * d + 12, 128 * m : 128 * (m + 1)
            ]
        out_ref[place, 100:104] = counts


def last_kernel(block_ref, input_out, hidden_out):
    total = jnp.sum(block_ref[...], axis=0)
    for out, first, rows, tiles, repeat in (
        (input_out, 64, 12, 3, PROBES),
        (hidden_out, 0, 32, 2, HPROBES),
    ):
        for m in range(tiles):
            owner = (lax.broadcasted_iota(jnp.int32, (1, 128), 1) + 128 * m) // repeat
            counts = jnp.zeros((1, 128), jnp.float32)
            for e in range(EXPERTS):
                counts = jnp.where(owner == e, total[100:101, e : e + 1], counts)
            out[:, 128 * m : 128 * (m + 1)] = total[first + rows * m : first + rows * (m + 1)] / counts


def call(kernel, out_shape, in_specs, out_specs, flops, size, limit=LIMIT, **kw):
    return pl.pallas_call(
        kernel,
        out_shape=out_shape,
        in_specs=in_specs,
        out_specs=out_specs,
        compiler_params=pltpu.CompilerParams(vmem_limit_bytes=limit),
        cost_estimate=pl.CostEstimate(flops=flops, bytes_accessed=size, transcendentals=0),
        **kw,
    )


def shape(*dims):
    return jax.ShapeDtypeStruct(dims, jnp.float32)


def body(inputs, expert_ids, hidden_grads, input_probes, hidden_probes):
    tokens = inputs.shape[0]
    core = lax.axis_index("tensor") % 2
    dp = jnp.arange(64, dtype=jnp.int32)
    x, zh, y = dp // 16, dp // 4 % 4, dp % 4
    place = jnp.where(core == 0, (x * 4 + y) * 4 + zh, (y * 4 + x) * 4 + zh)
    bf16 = jnp.bfloat16
    ids_pair = expert_ids.T
    ids_row = expert_ids.reshape(1, 2 * tokens)

    bf16 = jnp.bfloat16
    view = hidden_grads.reshape(tokens, 2, 16, 128).transpose(0, 2, 1, 3).reshape(tokens, 32, 128)
    send = call(
        norm_kernel,
        shape(8, 8, tokens),
        [HBM] * 3,
        VMEM,
        10**9,
        5 * 10**6,
        63 * 10**6,
        scratch_shapes=[
            pltpu.VMEM((tokens, 32, 128), bf16),
            pltpu.VMEM((tokens, 768), bf16),
            pltpu.VMEM((PROBES, 768), bf16),
            DMA((6,)),
        ],
    )(view, inputs, input_probes.T)
    got = lax.all_to_all(send, "tensor", 0, 0)
    rows, hproj = call(
        grads_kernel,
        (jax.ShapeDtypeStruct((8, 2 * tokens, 256), bf16), shape(HPROBES, 2 * tokens)),
        [HBM] * 2,
        (HBM, VMEM),
        4 * 10**9,
        9 * 10**6,
        55 * 10**6,
        scratch_shapes=[
            pltpu.VMEM((tokens, 32, 128), bf16),
            pltpu.VMEM((8, 2 * tokens, 256), bf16),
            pltpu.VMEM((HPROBES, 2048), bf16),
            DMA((5,)),
            DMA((4,)),
        ],
    )(view, hidden_probes.T)
    got, hproj = lax.optimization_barrier((got, hproj))
    send = call(between_kernel, shape(8, 8, tokens), [VMEM], VMEM, 10**5, 10**5)(got)
    everyone = lax.all_to_all(send, "tensor", 0, 0)
    block = call(
        hidden_kernel,
        shape(64, 104, 128),
        [SMEM] + [VMEM] * 4,
        VMEM,
        10**9,
        6 * 10**6,
    )(place, got, hproj, ids_row, rows)
    block = call(
        input_kernel,
        shape(64, 104, 128),
        [SMEM] + [VMEM] * 4,
        VMEM,
        10**9,
        3 * 10**6,
        input_output_aliases={4: 0},
    )(place, everyone, ids_pair, inputs, block)
    block = swap(block.reshape(4, 16, 104, 128), ring_groups(True))
    block = (block[0] + block[1]) + (block[2] + block[3])
    block = jnp.sum(swap(block.reshape(4, 4, 104, 128), ring_groups(False)), axis=0)
    block = swap(block, zh_groups())
    return call(
        last_kernel, (shape(12, 384), shape(32, 256)), [VMEM], (VMEM, VMEM), 10**5, 10**5
    )(block)


def solution(mesh):
    return jax.shard_map(
        body,
        mesh=mesh,
        in_specs=(
            P("dp", "tensor"),
            P("dp", None),
            P("dp", None, "tensor"),
            P("tensor", None),
            P("tensor", None),
        ),
        out_specs=(P(("tensor", "dp"), None), P(("tensor", "dp"), None)),
        check_vma=False,
    )
```

```python
import jax
import jax.numpy as jnp
from jax import lax
from jax.experimental import pallas as pl
from jax.experimental.pallas import tpu as pltpu
from jax.sharding import PartitionSpec as P

FF = 16384
EXPERTS = 8
PROBES = 48
HPROBES = 32
EPS = 1e-06
AXES = ("dp", "tensor")
LIMIT = 40 * 10**6
VMEM = pl.BlockSpec(memory_space=pltpu.VMEM)
SMEM = pl.BlockSpec(memory_space=pltpu.SMEM)
HBM = pl.BlockSpec(memory_space=pltpu.HBM)
DMA = pltpu.SemaphoreType.DMA


def linear(x, zh, y, t):
    return ((x * 4 + zh) * 4 + y) * 8 + t


def ring_groups(first):
    groups = []
    for zh in range(4):
        for t in range(8):
            along_x = (t % 2 == 1) == first
            for other in range(4):
                groups.append(
                    [linear(i, zh, other, t) if along_x else linear(other, zh, i, t) for i in range(4)]
                )
    return groups


def zh_groups():
    return [
        [linear(x, zh, y, t) for zh in range(4)] for x in range(4) for y in range(4) for t in range(8)
    ]


def swap(block, groups):
    return lax.all_to_all(block, AXES, 0, 0, axis_index_groups=groups)


def nt(left, right, **kw):
    return lax.dot_general(
        left, right, (((1,), (1,)), ((), ())), preferred_element_type=jnp.float32, **kw
    )


def pick_matrix():
    row = lax.broadcasted_iota(jnp.int32, (256, 64), 0)
    column = lax.broadcasted_iota(jnp.int32, (256, 64), 1)
    same = ((row >> 3) == (column >> 1)) & ((row & 1) == (column & 1))
    return jnp.where(same, 1.0, 0.0).astype(jnp.bfloat16)


def thirds(value):
    high = value.astype(jnp.bfloat16).astype(jnp.float32)
    middle = (value - high).astype(jnp.bfloat16).astype(jnp.float32)
    rest = value - high - middle
    return jnp.concatenate([high, middle, rest, jnp.zeros_like(value)], axis=0).astype(jnp.bfloat16)


def norm_kernel(view_hbm, inputs_hbm, probes_hbm, send_ref, view_ref, inputs_ref, probes_ref, sems):
    loads = [
        pltpu.make_async_copy(
            view_hbm.at[pl.ds(128 * c, 128)], view_ref.at[pl.ds(128 * c, 128)], sems.at[c]
        )
        for c in range(4)
    ]
    loads += [
        pltpu.make_async_copy(inputs_hbm, inputs_ref, sems.at[4]),
        pltpu.make_async_copy(probes_hbm, probes_ref, sems.at[5]),
    ]
    for load in loads:
        load.start()
    ones = jnp.ones((8, 128), jnp.bfloat16)
    sums = []
    for c in range(4):
        loads[c].wait()
        wide = view_ref[128 * c : 128 * c + 128].astype(jnp.float32)
        wide = wide * wide
        part = (wide[:, 0:8] + wide[:, 8:16]) + (wide[:, 16:24] + wide[:, 24:32])
        part = part.reshape(1024, 128)
        high = part.astype(jnp.bfloat16)
        low = (part - high.astype(jnp.float32)).astype(jnp.bfloat16)
        sums.append((nt(ones, high) + nt(ones, low))[0:1])
    lanes = thirds(jnp.concatenate(sums, axis=1))
    pick = pick_matrix()
    picked = [
        jnp.dot(lanes[:, 256 * b : 256 * (b + 1)], pick, preferred_element_type=jnp.float32)
        for b in range(16)
    ]
    picked = jnp.sum(jnp.concatenate(picked, axis=1), axis=0, keepdims=True)
    for t in range(8):
        send_ref[t, 6:7] = picked[:, 0:512]
        send_ref[t, 7:8] = picked[:, 512:1024]
    loads[4].wait()
    loads[5].wait()
    proj = nt(probes_ref[...], inputs_ref[...])
    for t in range(8):
        send_ref[t, 0:6] = proj[6 * t : 6 * t + 6]


def order_matrix():
    row = lax.broadcasted_iota(jnp.int32, (256, 256), 0)
    column = lax.broadcasted_iota(jnp.int32, (256, 256), 1)
    source = ((row >> 1) & 7) * 32 + (row >> 4) * 2 + (row & 1)
    return jnp.where(column == source, 1.0, 0.0).astype(jnp.bfloat16)


def grads_kernel(
    view_hbm, hprobes_hbm, rows_hbm, hproj_ref, view_ref, rows_ref, hprobes_ref, sems, out_sems
):
    loads = [
        pltpu.make_async_copy(
            view_hbm.at[pl.ds(128 * c, 128)], view_ref.at[pl.ds(128 * c, 128)], sems.at[c]
        )
        for c in range(4)
    ]
    probe_load = pltpu.make_async_copy(hprobes_hbm, hprobes_ref, sems.at[4])
    for load in loads:
        load.start()
    probe_load.start()
    order = order_matrix()
    stores = []
    for c in range(4):
        loads[c].wait()

        def step(i, carry):
            for half in range(4):
                first = i * 8 + half * 2
                pair = jnp.concatenate(
                    [view_ref[pl.ds((first + m) * 8, 8)].reshape(256, 128) for m in range(2)], axis=1
                )
                ordered = jnp.dot(order, pair, preferred_element_type=jnp.float32)
                for m in range(2):
                    at = pl.multiple_of((first + m) * 16, 16)
                    for tile in range(16):
                        piece = ordered[16 * tile : 16 * tile + 16, 128 * m : 128 * (m + 1)]
                        lanes = 128 * (tile % 2)
                        rows_ref[tile // 2, pl.ds(at, 16), lanes : lanes + 128] = piece.astype(
                            jnp.bfloat16
                        )
            return carry

        lax.fori_loop(2 * c, 2 * c + 2, step, 0)
        here = pl.ds(256 * c, 256)
        store = pltpu.make_async_copy(rows_ref.at[:, here], rows_hbm.at[:, here], out_sems.at[c])
        store.start()
        stores.append(store)
        if c == 0:
            probe_load.wait()
        total = jnp.zeros((HPROBES, 256), jnp.float32)
        for b in range(8):
            total = total + nt(
                hprobes_ref[:, 256 * b : 256 * (b + 1)], rows_ref[b, 256 * c : 256 * c + 256]
            )
        hproj_ref[:, 256 * c : 256 * c + 256] = total
    for store in stores:
        store.wait()


def between_kernel(got_ref, send_ref):
    mine = jnp.sum(got_ref[...], axis=0)
    for t in range(8):
        send_ref[t] = mine


def hidden_kernel(place_ref, got_ref, hproj_ref, ids_ref, rows_ref, out_ref):
    got = jnp.sum(got_ref[...], axis=0)
    squares = jnp.concatenate([got[6:7], got[7:8]], axis=1)
    scaled = hproj_ref[...] * jnp.minimum(1.0, FF / (squares + EPS))
    ids = ids_ref[...]
    weights = jnp.concatenate(
        [jnp.where(ids == e, scaled, 0.0).astype(jnp.bfloat16) for e in range(EXPERTS)], axis=0
    )
    for b in range(8):
        product = jnp.dot(
            weights, rows_ref[b], preferred_element_type=jnp.float32
        ).T
        for c in range(8):
            place = place_ref[8 * b + c]
            out_ref[place, 0:32] = product[32 * c : 32 * c + 32, 0:128]
            out_ref[place, 32:64] = product[32 * c : 32 * c + 32, 128:256]


def input_kernel(place_ref, everyone_ref, ids_ref, inputs_ref, partly_ref, out_ref):
    del partly_ref
    projected = jnp.concatenate([everyone_ref[t, 0:6] for t in range(8)], axis=0)
    ids = ids_ref[...]
    routed = [(ids[0:1] == e) | (ids[1:2] == e) for e in range(EXPERTS)]
    weights = jnp.concatenate(
        [jnp.where(r, projected, 0.0).astype(jnp.bfloat16) for r in routed], axis=0
    )
    product = jnp.dot(weights, inputs_ref[...], preferred_element_type=jnp.float32).T
    lane = lax.broadcasted_iota(jnp.int32, (4, 128), 1)
    counts = jnp.zeros((4, 128), jnp.float32)
    for e in range(EXPERTS):
        total = jnp.sum(jnp.where(routed[e], 1.0, 0.0), axis=1, keepdims=True)
        counts = jnp.where(lane == e, total, counts)
    for d in range(64):
        place = place_ref[d]
        for m in range(3):
            out_ref[place, 64 + 12 * m : 76 + 12 * m] = product[
                12 * d : 12 * d + 12, 128 * m : 128 * (m + 1)
            ]
        out_ref[place, 100:104] = counts


def last_kernel(block_ref, input_out, hidden_out):
    total = jnp.sum(block_ref[...], axis=0)
    for out, first, rows, tiles, repeat in (
        (input_out, 64, 12, 3, PROBES),
        (hidden_out, 0, 32, 2, HPROBES),
    ):
        for m in range(tiles):
            owner = (lax.broadcasted_iota(jnp.int32, (1, 128), 1) + 128 * m) // repeat
            counts = jnp.zeros((1, 128), jnp.float32)
            for e in range(EXPERTS):
                counts = jnp.where(owner == e, total[100:101, e : e + 1], counts)
            out[:, 128 * m : 128 * (m + 1)] = total[first + rows * m : first + rows * (m + 1)] / counts


def call(kernel, out_shape, in_specs, out_specs, flops, size, limit=LIMIT, **kw):
    return pl.pallas_call(
        kernel,
        out_shape=out_shape,
        in_specs=in_specs,
        out_specs=out_specs,
        compiler_params=pltpu.CompilerParams(vmem_limit_bytes=limit),
        cost_estimate=pl.CostEstimate(flops=flops, bytes_accessed=size, transcendentals=0),
        **kw,
    )


def shape(*dims):
    return jax.ShapeDtypeStruct(dims, jnp.float32)


def body(inputs, expert_ids, hidden_grads, input_probes, hidden_probes):
    tokens = inputs.shape[0]
    core = lax.axis_index("tensor") % 2
    dp = jnp.arange(64, dtype=jnp.int32)
    x, zh, y = dp // 16, dp // 4 % 4, dp % 4
    place = jnp.where(core == 1, (x * 4 + y) * 4 + zh, (y * 4 + x) * 4 + zh)
    bf16 = jnp.bfloat16
    ids_pair = expert_ids.T
    ids_row = expert_ids.reshape(1, 2 * tokens)

    bf16 = jnp.bfloat16
    view = hidden_grads.reshape(tokens, 2, 16, 128).transpose(0, 2, 1, 3).reshape(tokens, 32, 128)
    send = call(
        norm_kernel,
        shape(8, 8, tokens),
        [HBM] * 3,
        VMEM,
        10**9,
        5 * 10**6,
        63 * 10**6,
        scratch_shapes=[
            pltpu.VMEM((tokens, 32, 128), bf16),
            pltpu.VMEM((tokens, 768), bf16),
            pltpu.VMEM((PROBES, 768), bf16),
            DMA((6,)),
        ],
    )(view, inputs, input_probes.T)
    got = lax.all_to_all(send, "tensor", 0, 0)
    rows, hproj = call(
        grads_kernel,
        (jax.ShapeDtypeStruct((8, 2 * tokens, 256), bf16), shape(HPROBES, 2 * tokens)),
        [HBM] * 2,
        (HBM, VMEM),
        4 * 10**9,
        9 * 10**6,
        55 * 10**6,
        scratch_shapes=[
            pltpu.VMEM((tokens, 32, 128), bf16),
            pltpu.VMEM((8, 2 * tokens, 256), bf16),
            pltpu.VMEM((HPROBES, 2048), bf16),
            DMA((5,)),
            DMA((4,)),
        ],
    )(view, hidden_probes.T)
    got, hproj = lax.optimization_barrier((got, hproj))
    send = call(between_kernel, shape(8, 8, tokens), [VMEM], VMEM, 10**5, 10**5)(got)
    everyone = lax.all_to_all(send, "tensor", 0, 0)
    block = call(
        hidden_kernel,
        shape(64, 104, 128),
        [SMEM] + [VMEM] * 4,
        VMEM,
        10**9,
        6 * 10**6,
    )(place, got, hproj, ids_row, rows)
    block = call(
        input_kernel,
        shape(64, 104, 128),
        [SMEM] + [VMEM] * 4,
        VMEM,
        10**9,
        3 * 10**6,
        input_output_aliases={4: 0},
    )(place, everyone, ids_pair, inputs, block)
    block = swap(block.reshape(4, 16, 104, 128), ring_groups(True))
    block = (block[0] + block[1]) + (block[2] + block[3])
    block = jnp.sum(swap(block.reshape(4, 4, 104, 128), ring_groups(False)), axis=0)
    block = swap(block, zh_groups())
    return call(
        last_kernel, (shape(12, 384), shape(32, 256)), [VMEM], (VMEM, VMEM), 10**5, 10**5
    )(block)


def solution(mesh):
    return jax.shard_map(
        body,
        mesh=mesh,
        in_specs=(
            P("dp", "tensor"),
            P("dp", None),
            P("dp", None, "tensor"),
            P("tensor", None),
            P("tensor", None),
        ),
        out_specs=(P(("tensor", "dp"), None), P(("tensor", "dp"), None)),
        check_vma=False,
    )
```
